32 devices in a mesh: groups: 2 (over x), store: 16 (over z, y, core).
Axes of the slice: x: 2, y: 2, z: 4, core: 2. Of those that a mesh axis runs over, the one named last changes fastest.
Arguments:
- sources: bfloat16 [16384, 512], P(('groups', 'store')), parts along dimension 0, may hold values from -1800 to 1800
- self_terms: float32 [2, 8192], P(None, 'store'), may hold values from 0.5 to 2
- near_tiles: bfloat16 [2, 32, 5, 256, 256], P(None, 'store'), may hold values from -1 to 1
- near_cols: int32 [32, 5], P('store'), may hold values from 0 to 31, as said below
- near_count: int32 [32], P('store'), may hold values from 1 to 5, as said below
- far_cols: int32 [32, 6], P('store'), may hold values from 0 to 31, as said below
- basis_left: bfloat16 [32, 256, 32], P('store'), may hold values from -2 to 2
- basis_right: bfloat16 [32, 256, 32], P('store'), may hold values from -2 to 2
- couplings: bfloat16 [2, 32, 6, 32, 32], P(None, 'store'), may hold values from -1 to 1
Outputs:
- images: float32 [2, 16384, 512], P(None, ('groups', 'store')), parts along dimension 1
- heights: float32 [4, 512], P('groups'), parts along dimension 0
- norms: float32 [4, 512], P('groups'), parts along dimension 0
The draws below stay inside these ranges and needn't reach their ends.
There are 2 independent parts, one for each index of `groups`. The reference program is written for one: setup_inputs(seed, part) draws one part's arguments, and reference() takes and returns one part's arrays. A program takes and returns all parts, laid end to end along the dimension named above; an argument that names none is the same for every part. Nothing has to cross between parts.
Inputs may be any that keep to these rules, and one draw needn't show every extreme that they name: `near_cols`: the slots of row block i name the blocks i - 2 to i + 2, cyclically, each once, in a drawn order. Slots 0 to near_count - 1 of a row block are live; block 0 has all 5. `far_cols`: a far-field block lies more than 2 blocks from its row block, cyclically.
All inputs are finite; a program needn't handle non-finite values.
Results may differ from the reference program's by a relative error of at most 0.011.
Values may be sent and summed in bfloat16 or wider, within the bound.
A program may use at most 128 MiB of HBM per device.

```python
import math
import jax
import jax.numpy as jnp
from jax import lax

BLOCK = 256
SOURCES = 512
RANK = 32
REACH = 2
FAR = 6
NEAR = 5
BLOCKS = 32
PANELS = 8192


def draw_sources(key, part):
    key_rows = jax.random.fold_in(key, 0)
    key_cols = jax.random.fold_in(key, 1)
    key_base = jax.random.fold_in(key, 2)
    key_level = jax.random.fold_in(key, 4)
    key_sign = jax.random.fold_in(key, 5)
    key_block = jax.random.fold_in(key, 6)
    position = jnp.arange(PANELS, dtype=jnp.float32) / PANELS
    row_scale = jnp.exp(position * math.log(3.0)) * jnp.exp(jax.random.uniform(key_rows, (PANELS,)) * math.log(10.0))
    col_scale = jnp.exp(jax.random.uniform(key_cols, (SOURCES,)) * math.log(10.0))
    level = 0.7 + 0.6 * jax.random.uniform(key_level, (SOURCES,))
    signs = jnp.where(jax.random.bernoulli(key_sign, 0.5, (SOURCES,)), 1.0, -1.0)
    shared = (signs * level)[None, :]
    block_part = 0.5 * jax.random.normal(key_block, (BLOCKS, 1, SOURCES))
    block_part = jnp.broadcast_to(block_part, (BLOCKS, BLOCK, SOURCES)).reshape(PANELS, SOURCES)
    noise = jax.random.normal(key_base, (PANELS, SOURCES))
    draws_base = 0.6 * noise + shared + block_part
    values = jnp.clip(draws_base, -6.0, 6.0) * row_scale[:, None] * col_scale[None, :]
    return values.astype(jnp.bfloat16)


def draw_near_tiles(key, part):
    key_noise, key_level = jax.random.split(jax.random.fold_in(key, 21), 2)
    spread = 1.0 / math.sqrt(NEAR * BLOCK)
    level = 0.5 / BLOCK * (0.5 + jax.random.uniform(key_level, (2, BLOCKS, NEAR, 1, 1)))
    noise = jnp.clip(jax.random.normal(key_noise, (2, BLOCKS, NEAR, BLOCK, BLOCK)), -4.0, 4.0)
    return (level + spread * noise).astype(jnp.bfloat16)


def basis_draw(key, width):
    key_noise, key_mono = jax.random.split(key, 2)
    spread = 1.0 / math.sqrt(width)
    noise = jnp.clip(jax.random.normal(key_noise, (BLOCKS, BLOCK, RANK)), -4.0, 4.0) * spread
    mono = spread * (0.75 + 0.5 * jax.random.uniform(key_mono, (BLOCKS, BLOCK, RANK)))
    first_col = (jnp.arange(RANK, dtype=jnp.int32) == 0)[None, None, :]
    return jnp.where(first_col, mono, noise).astype(jnp.bfloat16)


def draw_basis_left(key, part):
    return basis_draw(jax.random.fold_in(key, 31), RANK)


def draw_basis_right(key, part):
    return basis_draw(jax.random.fold_in(key, 41), BLOCK)


def draw_couplings(key, part):
    key_noise, key_mono = jax.random.split(jax.random.fold_in(key, 51), 2)
    spread = 1.0 / math.sqrt(FAR * RANK)
    shape_all = (2, BLOCKS, FAR, RANK, RANK)
    noise = jnp.clip(jax.random.normal(key_noise, shape_all), -4.0, 4.0) * spread
    rows_at = jnp.arange(RANK, dtype=jnp.int32)[:, None]
    cols_at = jnp.arange(RANK, dtype=jnp.int32)[None, :]
    column_zero = cols_at == 0
    noise = jnp.where(column_zero, noise / math.sqrt(BLOCK), noise)
    mono_level = 0.6 * math.sqrt(RANK) / (FAR * math.sqrt(BLOCK))
    mono = mono_level * (0.5 + jax.random.uniform(key_mono, shape_all))
    corner = (rows_at == 0) & column_zero
    return jnp.where(corner, mono, noise).astype(jnp.bfloat16)


def draw_near_cols(key, part):
    scores = jax.random.randint(key, (BLOCKS, NEAR), 0, 1 << 20) * NEAR + jnp.arange(NEAR, dtype=jnp.int32)[None, :]
    orders = jnp.argsort(scores, axis=1).astype(jnp.int32)
    rows_at = jnp.arange(BLOCKS, dtype=jnp.int32)[:, None]
    return ((rows_at + orders - REACH) % BLOCKS).astype(jnp.int32)


def draw_near_count(key, part):
    key_first, key_second = jax.random.split(jax.random.fold_in(key, 7), 2)
    first_draw = jax.random.randint(key_first, (BLOCKS,), 1, NEAR + 1)
    second_draw = jax.random.randint(key_second, (BLOCKS,), 1, NEAR + 1)
    counts = jnp.minimum(first_draw, second_draw).at[0].set(NEAR)
    return counts.astype(jnp.int32)


def draw_far_cols(key, part):
    offsets = jax.random.randint(jax.random.fold_in(key, 11), (BLOCKS, FAR), REACH + 1, BLOCKS - REACH)
    rows_at = jnp.arange(BLOCKS, dtype=jnp.int32)[:, None]
    return ((rows_at + offsets) % BLOCKS).astype(jnp.int32)


def level_of(key, dims, shards, low, high):
    loudness = 1.0
    for axis_at, parts in shards:
        draws = jax.random.uniform(jax.random.fold_in(jax.random.fold_in(key, 6), axis_at), (parts,), jnp.float32, low / len(shards), high / len(shards))
        loudness = loudness * jnp.repeat(jnp.exp(draws), dims[axis_at] // parts).reshape((-1,) + (1,) * (len(dims) - 1 - axis_at))
    return loudness


def setup_inputs(seed: int = 0, part: int = 0) -> dict:
    streams_of = jax.random.split(jax.random.key(seed), 10)
    part_splits = jax.random.split(jax.random.fold_in(streams_of[9], part), 10)
    sources = draw_sources(jax.random.fold_in(jax.random.fold_in(streams_of[9], part), 71), part)
    self_terms = jnp.clip(jnp.exp(math.log(2.0) - 1.3862944 * jax.random.uniform(streams_of[1], (2, PANELS), jnp.float32) ** level_of(streams_of[1], (2, PANELS), ((1, 16),), -0.2, 0.2)), 0.5, 2.0)
    near_tiles = draw_near_tiles(jax.random.fold_in(streams_of[9], 71), part)
    near_cols = draw_near_cols(jax.random.fold_in(streams_of[9], 71), part)
    near_count = draw_near_count(jax.random.fold_in(streams_of[9], 71), part)
    far_cols = draw_far_cols(jax.random.fold_in(streams_of[9], 71), part)
    basis_left = draw_basis_left(jax.random.fold_in(streams_of[9], 71), part)
    basis_right = draw_basis_right(jax.random.fold_in(streams_of[9], 71), part)
    couplings = draw_couplings(jax.random.fold_in(streams_of[9], 71), part)
    return {"sources": sources, "self_terms": self_terms, "near_tiles": near_tiles, "near_cols": near_cols, "near_count": near_count, "far_cols": far_cols, "basis_left": basis_left, "basis_right": basis_right, "couplings": couplings}


EPSILON = 1e-06

def apply_operator(inputs, self_terms, near_tiles, near_cols, near_count, far_cols, basis_left, basis_right, couplings):
    coeffs = jnp.einsum('bpr,kbps->kbrs', basis_right.astype(jnp.float32), inputs.astype(jnp.float32)).astype(jnp.bfloat16)
    slot_ids = jnp.arange(NEAR, dtype=jnp.int32)

    def one_block(row_id):
        tiles_row = near_tiles[:, row_id].astype(jnp.float32)
        taken = inputs[:, near_cols[row_id]].astype(jnp.float32)
        weight = (slot_ids < near_count[row_id]).astype(jnp.float32)
        taken = taken * weight[None, :, None, None]
        taken = jnp.broadcast_to(taken, (2,) + taken.shape[1:])
        near_part = jnp.einsum('okpq,okqs->ops', tiles_row, taken)
        picked = coeffs[:, far_cols[row_id]].astype(jnp.float32)
        picked = jnp.broadcast_to(picked, (2,) + picked.shape[1:])
        reduced = jnp.einsum('ofrq,ofqs->ors', couplings[:, row_id].astype(jnp.float32), picked).astype(jnp.bfloat16)
        far_part = jnp.einsum('pr,ors->ops', basis_left[row_id].astype(jnp.float32), reduced.astype(jnp.float32)).astype(jnp.bfloat16)
        return near_part + far_part.astype(jnp.float32)
    rows_out = lax.map(one_block, jnp.arange(BLOCKS, dtype=jnp.int32))
    diagonal = self_terms.reshape(2, BLOCKS, BLOCK)
    return jnp.transpose(rows_out, (1, 0, 2, 3)) + diagonal[..., None] * inputs.astype(jnp.float32)

def reference(sources, self_terms, near_tiles, near_cols, near_count, far_cols, basis_left, basis_right, couplings):
    operands = (self_terms, near_tiles, near_cols, near_count, far_cols, basis_left, basis_right, couplings)
    source_f = sources.astype(jnp.float32).reshape(BLOCKS, BLOCK, SOURCES)
    scale_sq = lax.optimization_barrier(jnp.sum(source_f * source_f, axis=(0, 1))) / PANELS
    first_vec = (source_f / jnp.sqrt(scale_sq + EPSILON)).astype(jnp.bfloat16)
    image_one = apply_operator(first_vec[None], *operands)
    first_f = first_vec.astype(jnp.float32)
    heights = lax.optimization_barrier(jnp.sum(first_f[None] * image_one, axis=(1, 2))) / PANELS
    remain = image_one - heights[:, None, None, :] * first_f[None]
    norms = jnp.sqrt(lax.optimization_barrier(jnp.sum(remain * remain, axis=(1, 2))) / PANELS + EPSILON)
    second_vec = (remain / norms[:, None, None, :]).astype(jnp.bfloat16)
    image_two = apply_operator(second_vec, *operands)
    return (image_two.reshape(2, PANELS, SOURCES), heights, norms)
```

```python
import functools

import jax
import jax.numpy as jnp
from jax import lax
from jax.experimental import pallas as pl
from jax.experimental.pallas import tpu as pltpu
from jax.sharding import PartitionSpec as P

REACH = 2
EPSILON = 1e-06
CHUNK = 256
CORES = 2
TINY = 1e-30
MESH = pl.DeviceIdType.MESH
F32 = jnp.float32
BF16 = jnp.bfloat16


def kernel(
    devices,
    cols_ref,
    count_ref,
    far_ref,
    src_ref,
    self_ref,
    tiles_ref,
    left_ref,
    right_ref,
    coup_ref,
    out_ref,
    heights_ref,
    norms_ref,
    w_ref,
    g_ref,
    self_col,
    u1,
    u2,
    z1,
    z2,
    zsel,
    y_ref,
    stats,
    h1_send,
    h1_recv,
    h2_send,
    h2_recv,
    z1_send,
    z1_fsend,
    z1_recv,
    z2_send,
    z2_fsend,
    z2_recv,
    st_send,
    st_recv,
):
    me = lax.axis_index("store")
    chips = devices // CORES
    chip = me // CORES
    core = me % CORES
    partner = chip * CORES + (1 - core)
    right = (me + 1) % devices
    left = (me + devices - 1) % devices
    local = tiles_ref.shape[1]
    near = tiles_ref.shape[2]
    size = tiles_ref.shape[3]
    far = coup_ref.shape[2]
    rank = coup_ref.shape[3]
    rows = local * size
    width = u1.shape[2]
    chunks = u1.shape[0]
    blocks = devices * local
    panels = blocks * size

    def remote(src, dst, send, recv, peer):
        return pltpu.make_async_remote_copy(
            src_ref=src,
            dst_ref=dst,
            send_sem=send,
            recv_sem=recv,
            device_id={"store": peer},
            device_id_type=MESH,
        )

    barrier = pltpu.get_barrier_semaphore()

    @pl.loop(1, devices)
    def _(t):
        pl.semaphore_signal(
            barrier, inc=1, device_id={"store": (me + t) % devices}, device_id_type=MESH
        )

    pl.semaphore_wait(barrier, devices - 1)

    def halo(field, c, send, recv):
        own = field.at[pl.ds(rows, rows)]
        return (
            remote(own, field.at[pl.ds(0, rows)], send.at[c, 0], recv.at[c, 0], right),
            remote(own, field.at[pl.ds(2 * rows, rows)], send.at[c, 1], recv.at[c, 1], left),
        )

    def coeff_copy(z, c, send, recv, source, peer):
        part = z[c].at[pl.ds(source * local, local)]
        return remote(part, part, send, recv.at[c, source], peer)

    def coeff_start(z, c, send, recv):
        coeff_copy(z, c, send.at[c, 0], recv, me, partner).start()

        @pl.loop(1, chips)
        def _(t):
            peer = ((chip + t) % chips) * CORES + core
            coeff_copy(z, c, send.at[c, t], recv, me, peer).start()

    def coeff_forward(z, c, fsend, recv):
        @pl.loop(1, chips)
        def _(t):
            source = ((chip + chips - t) % chips) * CORES + core
            copy = coeff_copy(z, c, fsend.at[c, t], recv, source, partner)
            copy.wait_recv()
            copy.start()

    def coeff_wait(z, c, fsend, recv):
        coeff_copy(z, c, fsend.at[c, 0], recv, partner, partner).wait_recv()

        @pl.loop(1, chips)
        def _(t):
            source = ((chip + chips - t) % chips) * CORES + (1 - core)
            coeff_copy(z, c, fsend.at[c, t], recv, source, partner).wait_recv()

    def coeff_drain(z, c, send, fsend, recv):
        coeff_copy(z, c, send.at[c, 0], recv, me, partner).wait_send()

        @pl.loop(1, chips)
        def _(t):
            coeff_copy(z, c, send.at[c, t], recv, me, partner).wait_send()
            coeff_copy(z, c, fsend.at[c, t], recv, me, partner).wait_send()

    def stat_copy(c, source, peer, t):
        part = stats.at[c, source]
        return remote(part, part, st_send.at[c, t], st_recv.at[c, source], peer)

    def to_coeffs(r, values):
        return lax.dot_general(
            right_ref[r], values, (((0,), (0,)), ((), ())), preferred_element_type=F32
        ).astype(BF16)

    for c in range(chunks):
        cut = pl.ds(c * width, width)
        u1[c, pl.ds(rows, rows)] = src_ref[:, cut]
        for copy in halo(u1.at[c], c, h1_send, h1_recv):
            copy.start()
        for r in range(local):
            z1[c][me * local + r] = to_coeffs(r, src_ref[pl.ds(r * size, size), cut])
        coeff_start(z1, c, z1_send, z1_recv)

    for r in range(local):
        row = me * local + r
        for d in range(near):
            target = (row + d - REACH + blocks) % blocks
            slot = jnp.int32(0)
            for k in range(1, near):
                slot = jnp.where(cols_ref[r, k] == target, k, slot)
            live = (slot < count_ref[r]).astype(F32).astype(BF16)
            for o in range(2):
                w_ref[o, r, :, pl.ds(d * size, size)] = tiles_ref[o, r, slot] * live
        for o in range(2):
            parts = [
                lax.dot_general(
                    coup_ref[o, r, k],
                    left_ref[r],
                    (((0,), (1,)), ((), ())),
                    preferred_element_type=F32,
                )
                for k in range(far)
            ]
            parts.append(jnp.zeros((g_ref.shape[3] - far * rank, size), F32))
            g_ref[o, r] = jnp.concatenate(parts, axis=0).T.astype(BF16)
        diag = lax.broadcasted_iota(jnp.int32, (size, size), 0) == lax.broadcasted_iota(
            jnp.int32, (size, size), 1
        )
        for o in range(2):
            line = self_ref[pl.ds(o, 1), pl.ds(r * size, size)]
            self_col[o, pl.ds(r * size, size)] = jnp.sum(
                jnp.where(diag, line, 0.0), axis=1, keepdims=True
            )
    zsel[...] = jnp.zeros_like(zsel)

    def product(o, r, field, z, c, offset):
        for k in range(far):
            zsel[r, pl.ds(k * rank, rank)] = z[c][far_ref[r, k], pl.ds(offset, rank)]
        total = jnp.dot(
            w_ref[o, r],
            field[pl.ds(r * size, near * size)],
            preferred_element_type=F32,
        )
        total += jnp.dot(g_ref[o, r], zsel[r], preferred_element_type=F32)
        own = field[pl.ds(rows + r * size, size)].astype(F32)
        return total + self_col[o, pl.ds(r * size, size)] * own, own

    def first(c):
        coeff_forward(z1, c, z1_fsend, z1_recv)
        coeff_wait(z1, c, z1_fsend, z1_recv)
        for copy in halo(u1.at[c], c, h1_send, h1_recv):
            copy.wait_recv()
        q = jnp.zeros((1, width), F32)
        p = [jnp.zeros((1, width), F32) for _ in range(2)]
        for r in range(local):
            for o in range(2):
                value, own = product(o, r, u1.at[c], z1, c, 0)
                y_ref[c, o, pl.ds(r * size, size)] = value
                p[o] += jnp.sum(value * own, axis=0, keepdims=True)
                if o == 0:
                    q += jnp.sum(own * own, axis=0, keepdims=True)
        h = [p[o] / jnp.maximum(q, TINY) for o in range(2)]
        rest = []
        for o in range(2):
            own = src_ref[:, pl.ds(c * width, width)].astype(F32)
            rem = y_ref[c, o] - h[o] * own
            rest.append(jnp.sum(rem * rem, axis=0, keepdims=True))
        zero = jnp.zeros((1, width), F32)
        stats[c, me] = jnp.concatenate([q, *p, *h, *rest, zero], axis=0)

        @pl.loop(1, devices)
        def _(t):
            stat_copy(c, me, (me + t) % devices, t).start()

    def second(c):
        @pl.loop(1, devices)
        def _(t):
            stat_copy(c, (me + devices - t) % devices, me, t).wait_recv()

        cut = pl.ds(c * width, width)
        every = stats[c]
        sums = jnp.sum(every, axis=0)
        scale = sums[0:1] / panels
        inv = 1.0 / jnp.sqrt(scale + EPSILON)
        own = src_ref[:, cut].astype(F32)
        root = jnp.sqrt(every[:, 0:1])
        for o in range(2):
            h = sums[1 + o : 2 + o] * inv * inv / panels
            off = (every[:, 3 + o : 4 + o] - h[None]) * root
            spread = (sums[5 + o : 6 + o] + jnp.sum(off * off, axis=0)) * inv * inv / panels
            norm = jnp.sqrt(spread + EPSILON)
            heights_ref[pl.ds(o, 1), cut] = h
            norms_ref[pl.ds(o, 1), cut] = norm
            value = ((y_ref[c, o] - h * own) * (inv / norm)).astype(BF16)
            u2[c, o, pl.ds(rows, rows)] = value
            for copy in halo(u2.at[c, o], 2 * c + o, h2_send, h2_recv):
                copy.start()
            for r in range(local):
                z2[c][me * local + r, pl.ds(o * rank, rank)] = to_coeffs(
                    r, value[r * size : (r + 1) * size]
                )
        coeff_start(z2, c, z2_send, z2_recv)

    def third(c):
        coeff_forward(z2, c, z2_fsend, z2_recv)
        coeff_wait(z2, c, z2_fsend, z2_recv)
        for o in range(2):
            for copy in halo(u2.at[c, o], 2 * c + o, h2_send, h2_recv):
                copy.wait_recv()
            for r in range(local):
                value, _ = product(o, r, u2.at[c, o], z2, c, o * rank)
                out_ref[o, pl.ds(r * size, size), pl.ds(c * width, width)] = value

    for c in range(chunks):
        first(c)
        if c >= 1:
            second(c - 1)
    second(chunks - 1)
    for c in range(chunks):
        third(c)

    for c in range(chunks):
        for copy in halo(u1.at[c], c, h1_send, h1_recv):
            copy.wait_send()
        for o in range(2):
            for copy in halo(u2.at[c, o], 2 * c + o, h2_send, h2_recv):
                copy.wait_send()
        coeff_drain(z1, c, z1_send, z1_fsend, z1_recv)
        coeff_drain(z2, c, z2_send, z2_fsend, z2_recv)

        @pl.loop(1, devices)
        def _(t):
            stat_copy(c, me, partner, t).wait_send()


def shards(
    devices,
    sources,
    self_terms,
    near_tiles,
    near_cols,
    near_count,
    far_cols,
    basis_left,
    basis_right,
    couplings,
):
    rows, columns = sources.shape
    local, near, size = near_tiles.shape[1:4]
    far, rank = couplings.shape[2:4]
    blocks = devices * local
    chunks = columns // CHUNK
    chips = devices // CORES
    depth = -(-far * rank // 128) * 128
    dma = pltpu.SemaphoreType.DMA
    smem = pl.BlockSpec(memory_space=pltpu.SMEM)
    vmem = pl.BlockSpec(memory_space=pltpu.VMEM)
    return pl.pallas_call(
        functools.partial(kernel, devices),
        out_shape=(
            jax.ShapeDtypeStruct((2, rows, columns), F32),
            jax.ShapeDtypeStruct((2, columns), F32),
            jax.ShapeDtypeStruct((2, columns), F32),
        ),
        in_specs=[smem] * 3 + [vmem] * 6,
        out_specs=(vmem,) * 3,
        scratch_shapes=[
            pltpu.VMEM((2, local, size, near * size), BF16),
            pltpu.VMEM((2, local, size, depth), BF16),
            pltpu.VMEM((2, rows, 1), F32),
            pltpu.VMEM((chunks, 3 * rows, CHUNK), BF16),
            pltpu.VMEM((chunks, 2, 3 * rows, CHUNK), BF16),
            [pltpu.VMEM((blocks, rank, CHUNK), BF16)] * chunks,
            [pltpu.VMEM((blocks, 2 * rank, CHUNK), BF16)] * chunks,
            pltpu.VMEM((local, depth, CHUNK), BF16),
            pltpu.VMEM((chunks, 2, rows, CHUNK), F32),
            pltpu.VMEM((chunks, devices, 8, CHUNK), F32),
            dma((chunks, 2)),
            dma((chunks, 2)),
            dma((2 * chunks, 2)),
            dma((2 * chunks, 2)),
            dma((chunks, chips)),
            dma((chunks, chips)),
            dma((chunks, devices)),
            dma((chunks, chips)),
            dma((chunks, chips)),
            dma((chunks, devices)),
            dma((chunks, devices)),
            dma((chunks, devices)),
        ],
        compiler_params=pltpu.CompilerParams(
            collective_id=0, has_side_effects=True, vmem_limit_bytes=56 * 1024 * 1024
        ),
    )(
        near_cols,
        near_count,
        far_cols,
        sources,
        self_terms,
        near_tiles,
        basis_left,
        basis_right,
        couplings,
    )


def solution(mesh):
    placed = (
        P(("groups", "store"), None),
        P(None, "store"),
        P(None, "store", None, None, None),
        P("store", None),
        P("store"),
        P("store", None),
        P("store", None, None),
        P("store", None, None),
        P(None, "store", None, None, None),
    )
    return jax.shard_map(
        functools.partial(shards, mesh.shape["store"]),
        mesh=mesh,
        in_specs=placed,
        out_specs=(P(None, ("groups", "store"), None), P("groups", None), P("groups", None)),
        check_vma=False,
    )
```

```python
import functools

import jax
import jax.numpy as jnp
from jax import lax
from jax.experimental import pallas as pl
from jax.experimental.pallas import tpu as pltpu
from jax.sharding import PartitionSpec as P

REACH = 2
EPSILON = 1e-06
CHUNK = 256
CORES = 2
TINY = 1e-30
MESH = pl.DeviceIdType.MESH
F32 = jnp.float32
BF16 = jnp.bfloat16


def kernel(
    devices,
    cols_ref,
    count_ref,
    far_ref,
    src_ref,
    self_ref,
    tiles_ref,
    left_ref,
    right_ref,
    coup_ref,
    out_ref,
    heights_ref,
    norms_ref,
    w_ref,
    g_ref,
    self_col,
    u1,
    u2,
    z1,
    z2,
    zsel,
    y_ref,
    stats,
    h1_send,
    h1_recv,
    h2_send,
    h2_recv,
    z1_send,
    z1_fsend,
    z1_recv,
    z2_send,
    z2_fsend,
    z2_recv,
    st_send,
    st_recv,
):
    me = lax.axis_index("store")
    chips = devices // CORES
    chip = me // CORES
    core = me % CORES
    partner = chip * CORES + (1 - core)
    right = (me + 1) % devices
    left = (me + devices - 1) % devices
    local = tiles_ref.shape[1]
    near = tiles_ref.shape[2]
    size = tiles_ref.shape[3]
    far = coup_ref.shape[2]
    rank = coup_ref.shape[3]
    rows = local * size
    width = u1.shape[2]
    chunks = u1.shape[0]
    blocks = devices * local
    panels = blocks * size

    def remote(src, dst, send, recv, peer):
        return pltpu.make_async_remote_copy(
            src_ref=src,
            dst_ref=dst,
            send_sem=send,
            recv_sem=recv,
            device_id={"store": peer},
            device_id_type=MESH,
        )

    barrier = pltpu.get_barrier_semaphore()

    @pl.loop(1, devices)
    def _(t):
        pl.semaphore_signal(
            barrier, inc=1, device_id={"store": (me + t) % devices}, device_id_type=MESH
        )

    pl.semaphore_wait(barrier, devices - 1)

    def halo(field, c, send, recv):
        own = field.at[pl.ds(rows, rows)]
        return (
            remote(own, field.at[pl.ds(0, rows)], send.at[c, 0], recv.at[c, 0], right),
            remote(own, field.at[pl.ds(2 * rows, rows)], send.at[c, 1], recv.at[c, 1], left),
        )

    def coeff_copy(z, c, send, recv, source, peer):
        part = z[c].at[pl.ds(source * local, local)]
        return remote(part, part, send, recv.at[c, source], peer)

    def coeff_start(z, c, send, recv):
        coeff_copy(z, c, send.at[c, 0], recv, me, partner).start()

        @pl.loop(1, chips)
        def _(t):
            peer = ((chip + t) % chips) * CORES + core
            coeff_copy(z, c, send.at[c, t], recv, me, peer).start()

    def coeff_forward(z, c, fsend, recv):
        @pl.loop(1, chips)
        def _(t):
            source = ((chip + chips - t) % chips) * CORES + core
            copy = coeff_copy(z, c, fsend.at[c, t], recv, source, partner)
            copy.wait_recv()
            copy.start()

    def coeff_wait(z, c, fsend, recv):
        coeff_copy(z, c, fsend.at[c, 0], recv, partner, partner).wait_recv()

        @pl.loop(1, chips)
        def _(t):
            source = ((chip + chips - t) % chips) * CORES + (1 - core)
            coeff_copy(z, c, fsend.at[c, t], recv, source, partner).wait_recv()

    def coeff_drain(z, c, send, fsend, recv):
        coeff_copy(z, c, send.at[c, 0], recv, me, partner).wait_send()

        @pl.loop(1, chips)
        def _(t):
            coeff_copy(z, c, send.at[c, t], recv, me, partner).wait_send()
            coeff_copy(z, c, fsend.at[c, t], recv, me, partner).wait_send()

    def stat_copy(c, source, peer, t):
        part = stats.at[c, source]
        return remote(part, part, st_send.at[c, t], st_recv.at[c, source], peer)

    def to_coeffs(r, values):
        return jnp.dot(right_ref[r], values, preferred_element_type=F32).astype(BF16)

    for c in range(chunks):
        cut = pl.ds(c * width, width)
        for r in range(local):
            z1[c][me * local + r] = to_coeffs(r, src_ref[pl.ds(r * size, size), cut])
        coeff_start(z1, c, z1_send, z1_recv)
    for c in range(chunks):
        u1[c, pl.ds(rows, rows)] = src_ref[:, pl.ds(c * width, width)]
        for copy in halo(u1.at[c], c, h1_send, h1_recv):
            copy.start()

    for r in range(local):
        row = me * local + r
        for d in range(near):
            target = (row + d - REACH + blocks) % blocks
            slot = jnp.int32(0)
            for k in range(1, near):
                slot = jnp.where(cols_ref[r, k] == target, k, slot)
            live = (slot < count_ref[r]).astype(F32).astype(BF16)
            for o in range(2):
                w_ref[o, r, :, pl.ds(d * size, size)] = tiles_ref[o, r, slot] * live
        for o in range(2):
            parts = [
                lax.dot_general(
                    coup_ref[o, r, k],
                    left_ref[r],
                    (((0,), (0,)), ((), ())),
                    preferred_element_type=F32,
                )
                for k in range(far)
            ]
            parts.append(jnp.zeros((g_ref.shape[3] - far * rank, size), F32))
            g_ref[o, r] = jnp.concatenate(parts, axis=0).T.astype(BF16)
        diag = lax.broadcasted_iota(jnp.int32, (size, size), 0) == lax.broadcasted_iota(
            jnp.int32, (size, size), 1
        )
        for o in range(2):
            line = self_ref[pl.ds(o, 1), pl.ds(r * size, size)]
            self_col[o, pl.ds(r * size, size)] = jnp.sum(
                jnp.where(diag, line, 0.0), axis=1, keepdims=True
            )
    zsel[...] = jnp.zeros_like(zsel)

    def product(o, r, field, z, c, offset):
        for k in range(far):
            zsel[r, pl.ds(k * rank, rank)] = z[c][far_ref[r, k], pl.ds(offset, rank)]
        total = jnp.dot(
            w_ref[o, r],
            field[pl.ds(r * size, near * size)],
            preferred_element_type=F32,
        )
        total += jnp.dot(g_ref[o, r], zsel[r], preferred_element_type=F32)
        own = field[pl.ds(rows + r * size, size)].astype(F32)
        return total + self_col[o, pl.ds(r * size, size)] * own, own

    def first(c):
        coeff_forward(z1, c, z1_fsend, z1_recv)
        coeff_wait(z1, c, z1_fsend, z1_recv)
        for copy in halo(u1.at[c], c, h1_send, h1_recv):
            copy.wait_recv()
        q = jnp.zeros((1, width), F32)
        p = [jnp.zeros((1, width), F32) for _ in range(2)]
        for r in range(local):
            for o in range(2):
                value, own = product(o, r, u1.at[c], z1, c, 0)
                y_ref[c, o, pl.ds(r * size, size)] = value
                p[o] += jnp.sum(value * own, axis=0, keepdims=True)
                if o == 0:
                    q += jnp.sum(own * own, axis=0, keepdims=True)
        h = [p[o] / jnp.maximum(q, TINY) for o in range(2)]
        rest = []
        for o in range(2):
            own = src_ref[:, pl.ds(c * width, width)].astype(F32)
            rem = y_ref[c, o] - h[o] * own
            rest.append(jnp.sum(rem * rem, axis=0, keepdims=True))
        zero = jnp.zeros((1, width), F32)
        stats[c, me] = jnp.concatenate([q, *p, *h, *rest, zero], axis=0)

        @pl.loop(1, devices)
        def _(t):
            stat_copy(c, me, (me + t) % devices, t).start()

    def second(c):
        @pl.loop(1, devices)
        def _(t):
            stat_copy(c, (me + devices - t) % devices, me, t).wait_recv()

        cut = pl.ds(c * width, width)
        every = stats[c]
        sums = jnp.sum(every, axis=0)
        scale = sums[0:1] / panels
        inv = 1.0 / jnp.sqrt(scale + EPSILON)
        own = src_ref[:, cut].astype(F32)
        root = jnp.sqrt(every[:, 0:1])
        for o in range(2):
            h = sums[1 + o : 2 + o] * inv * inv / panels
            off = (every[:, 3 + o : 4 + o] - h[None]) * root
            spread = (sums[5 + o : 6 + o] + jnp.sum(off * off, axis=0)) * inv * inv / panels
            norm = jnp.sqrt(spread + EPSILON)
            heights_ref[pl.ds(o, 1), cut] = h
            norms_ref[pl.ds(o, 1), cut] = norm
            value = ((y_ref[c, o] - h * own) * (inv / norm)).astype(BF16)
            u2[c, o, pl.ds(rows, rows)] = value
            for r in range(local):
                z2[c][me * local + r, pl.ds(o * rank, rank)] = to_coeffs(
                    r, value[r * size : (r + 1) * size]
                )
        coeff_start(z2, c, z2_send, z2_recv)
        for o in range(2):
            for copy in halo(u2.at[c, o], 2 * c + o, h2_send, h2_recv):
                copy.start()

    def third(c):
        coeff_forward(z2, c, z2_fsend, z2_recv)
        coeff_wait(z2, c, z2_fsend, z2_recv)
        for o in range(2):
            for copy in halo(u2.at[c, o], 2 * c + o, h2_send, h2_recv):
                copy.wait_recv()
            for r in range(local):
                value, _ = product(o, r, u2.at[c, o], z2, c, o * rank)
                out_ref[o, pl.ds(r * size, size), pl.ds(c * width, width)] = value

    for c in range(chunks):
        first(c)
        if c >= 1:
            second(c - 1)
    second(chunks - 1)
    for c in range(chunks):
        third(c)

    for c in range(chunks):
        for copy in halo(u1.at[c], c, h1_send, h1_recv):
            copy.wait_send()
        for o in range(2):
            for copy in halo(u2.at[c, o], 2 * c + o, h2_send, h2_recv):
                copy.wait_send()
        coeff_drain(z1, c, z1_send, z1_fsend, z1_recv)
        coeff_drain(z2, c, z2_send, z2_fsend, z2_recv)

        @pl.loop(1, devices)
        def _(t):
            stat_copy(c, me, partner, t).wait_send()


def hand_over(images_ref, heights_ref, norms_ref, out_images, out_heights, out_norms):
    out_images[...] = images_ref[...]
    out_heights[...] = heights_ref[...]
    out_norms[...] = norms_ref[...]


def shards(
    devices,
    sources,
    self_terms,
    near_tiles,
    near_cols,
    near_count,
    far_cols,
    basis_left,
    basis_right,
    couplings,
):
    rows, columns = sources.shape
    local, near, size = near_tiles.shape[1:4]
    far, rank = couplings.shape[2:4]
    blocks = devices * local
    chunks = columns // CHUNK
    chips = devices // CORES
    depth = -(-far * rank // 128) * 128
    dma = pltpu.SemaphoreType.DMA
    smem = pl.BlockSpec(memory_space=pltpu.SMEM)
    vmem = pl.BlockSpec(memory_space=pltpu.VMEM)
    results = pl.pallas_call(
        functools.partial(kernel, devices),
        out_shape=(
            jax.ShapeDtypeStruct((2, rows, columns), F32),
            jax.ShapeDtypeStruct((2, columns), F32),
            jax.ShapeDtypeStruct((2, columns), F32),
        ),
        in_specs=[smem] * 3 + [vmem] * 6,
        out_specs=(vmem,) * 3,
        scratch_shapes=[
            pltpu.VMEM((2, local, size, near * size), BF16),
            pltpu.VMEM((2, local, size, depth), BF16),
            pltpu.VMEM((2, rows, 1), F32),
            pltpu.VMEM((chunks, 3 * rows, CHUNK), BF16),
            pltpu.VMEM((chunks, 2, 3 * rows, CHUNK), BF16),
            [pltpu.VMEM((blocks, rank, CHUNK), BF16)] * chunks,
            [pltpu.VMEM((blocks, 2 * rank, CHUNK), BF16)] * chunks,
            pltpu.VMEM((local, depth, CHUNK), BF16),
            pltpu.VMEM((chunks, 2, rows, CHUNK), F32),
            pltpu.VMEM((chunks, devices, 8, CHUNK), F32),
            dma((chunks, 2)),
            dma((chunks, 2)),
            dma((2 * chunks, 2)),
            dma((2 * chunks, 2)),
            dma((chunks, chips)),
            dma((chunks, chips)),
            dma((chunks, devices)),
            dma((chunks, chips)),
            dma((chunks, chips)),
            dma((chunks, devices)),
            dma((chunks, devices)),
            dma((chunks, devices)),
        ],
        compiler_params=pltpu.CompilerParams(
            collective_id=0, has_side_effects=True, vmem_limit_bytes=56 * 1024 * 1024
        ),
    )(
        near_cols,
        near_count,
        far_cols,
        sources,
        self_terms,
        near_tiles,
        jnp.swapaxes(basis_left, 1, 2),
        jnp.swapaxes(basis_right, 1, 2),
        couplings,
    )
    specs = (
        pl.BlockSpec((1, rows // 2, columns), lambda o, k: (o, k, 0)),
        pl.BlockSpec((2, columns), lambda o, k: (0, 0)),
        pl.BlockSpec((2, columns), lambda o, k: (0, 0)),
    )
    return pl.pallas_call(
        hand_over,
        grid=(2, 2),
        out_shape=tuple(jax.ShapeDtypeStruct(r.shape, r.dtype) for r in results),
        in_specs=specs,
        out_specs=specs,
    )(*results)


def solution(mesh):
    placed = (
        P(("groups", "store"), None),
        P(None, "store"),
        P(None, "store", None, None, None),
        P("store", None),
        P("store"),
        P("store", None),
        P("store", None, None),
        P("store", None, None),
        P(None, "store", None, None, None),
    )
    return jax.shard_map(
        functools.partial(shards, mesh.shape["store"]),
        mesh=mesh,
        in_specs=placed,
        out_specs=(P(None, ("groups", "store"), None), P("groups", None), P("groups", None)),
        check_vma=False,
    )
```
